256 devices in a mesh: rcv: 16 (over y, x), src: 8 (over z), freq: 2 (over core).
Axes of the slice: x: 4, y: 4, z: 8, core: 2. Of those that a mesh axis runs over, the one named last changes fastest.
Arguments:
- slice_data: bfloat16 [4, 6144, 6144], P('freq', 'rcv', 'src'), parts along dimension 0, may hold values from -6 to 6
Outputs:
- multiples: float32 [4, 6144, 6144], P('freq', 'rcv', 'src'), parts along dimension 0
The draws below stay inside these ranges and needn't reach their ends.
There are 2 independent parts, one for each index of `freq`. The reference program is written for one: setup_inputs(seed, part) draws one part's arguments, and reference() takes and returns one part's arrays. A program takes and returns all parts, laid end to end along the dimension named above; each array names one. Nothing has to cross between parts.
All inputs are finite; a program needn't handle non-finite values.
Results may differ from the reference program's by a relative error of at most 0.0003.
Values may be sent and summed in bfloat16 or wider, within the bound.
No kernel may reach another device: no remote copies, remote signals or barrier semaphores. Data moves between devices by JAX's collectives and lax.ppermute only.
A program may use at most 128 MiB of HBM per device.

```python
import jax
import jax.numpy as jnp
from jax import lax

NR = 6144
NS = 6144


def block_levels(key, dims, cuts, smallest, high):
    gain, own = 1.0, jax.random.fold_in(key, 6)
    for position, blocks in cuts:
        heights = jnp.exp(jax.random.uniform(jax.random.fold_in(own, position), (blocks,), jnp.float32, smallest / len(cuts), high / len(cuts)))
        gain = gain * jnp.repeat(heights, dims[position] // blocks).reshape([-1 if axis == position else 1 for axis in range(len(dims))])
    return gain


def bell_draw(stream_key, dims, width, most, pieces=(), kind=jnp.bfloat16):
    loudness = block_levels(stream_key, dims, pieces, -0.22, 0.18) if pieces else 1.0
    values = jax.random.normal(stream_key, dims, jnp.float32) * width * loudness
    return jnp.minimum(jnp.maximum(values, -most), most).astype(kind)


def setup_inputs(seed: int = 0, part: int = 0) -> dict:
    seeds = jax.random.split(jax.random.key(seed), 2)
    part_splits = jax.random.split(jax.random.fold_in(seeds[1], part), 2)
    return {
        "slice_data": bell_draw(part_splits[0], (2, NR, NS), 1.0, 6.0, ((1, 16), (2, 8))),
    }


def reference(slice_data):
    data_re = slice_data[0]
    data_im = slice_data[1]
    blocks = NR // 512 if NR % 512 == 0 else 1
    rows_re = data_re.reshape(blocks, NR // blocks, NS)
    rows_im = data_im.reshape(blocks, NR // blocks, NS)
    scale = 1.0 / jnp.sqrt(jnp.float32(NS))

    def one_block(pair):
        left_re, left_im = pair
        real_part = jnp.dot(left_re, data_re, preferred_element_type=jnp.float32) - jnp.dot(left_im, data_im, preferred_element_type=jnp.float32)
        imag_part = jnp.dot(left_re, data_im, preferred_element_type=jnp.float32) + jnp.dot(left_im, data_re, preferred_element_type=jnp.float32)
        return jnp.stack([real_part * scale, imag_part * scale])
    result = lax.map(one_block, (rows_re, rows_im))
    return jnp.transpose(result, (1, 0, 2, 3)).reshape(2, NR, NS)
```

```python
import functools

import jax
import jax.numpy as jnp
from jax import lax
from jax.experimental import pallas as pl
from jax.experimental.pallas import tpu as pltpu
from jax.sharding import PartitionSpec as P

NS = 6144
WINDOW = 5


def plane_pairs(first, hop):
    pairs = []
    for y in range(4):
        for x in range(4):
            for core in range(2):
                if (core == 0) == first:
                    target = y * 4 + (x + hop) % 4
                else:
                    target = ((y + hop) % 4) * 4 + x
                pairs.append(((y * 4 + x) * 2 + core, target * 2 + core))
    return pairs


def ring_pairs(hop):
    return [(z * 2 + core, (z + (hop if core == 0 else -hop)) % 8 * 2 + core) for z in range(8) for core in range(2)]


STEPS = (
    ((-1, 0), (0, 0), "a", 1),
    ((1, 0), (0, 0), "a", -1),
    (-1, 0, "z", 1),
    ((2, 0), (-1, 0), "a", 1),
    ((0, 1), (0, 0), "b", -1),
    (1, 0, "z", -1),
    ((0, -1), (0, 0), "b", 1),
    ((-1, 1), (-1, 0), "b", -1),
    (-2, -1, "z", 1),
    ((-1, -1), (-1, 0), "b", 1),
    ((1, 1), (1, 0), "b", -1),
    (2, 1, "z", -1),
    ((1, -1), (1, 0), "b", 1),
    ((0, 2), (0, 1), "b", -1),
    (-3, -2, "z", 1),
    ((2, -1), (2, 0), "b", 1),
    ((2, 1), (2, 0), "b", -1),
    (3, 2, "z", -1),
    ((-1, 2), (-1, -1), "b", 1),
    ((1, 2), (1, 1), "b", -1),
    (4, -3, "z", 1),
    ((2, 2), (2, -1), "b", 1),
)
EARLY = [(0, 0)] + [step[0] for step in STEPS[:18] if step[2] != "z"]
LATE = [step[0] for step in STEPS[18:] if step[2] != "z"]
NEAR = (0, 1, 2, 3, -3, -2, -1)


def move(value, axis, hop):
    if axis == "z":
        return lax.ppermute(value, ("src", "freq"), ring_pairs(hop))
    return lax.ppermute(value, ("rcv", "freq"), plane_pairs(axis == "a", hop))


def place():
    here, row, core = lax.axis_index("src"), lax.axis_index("rcv"), lax.axis_index("freq")
    return here, row // 4, row % 4, core


def owner_of(key):
    _, y, x, core = place()
    a, b = key
    dx, dy = jnp.where(core == 0, a, b), jnp.where(core == 0, b, a)
    return ((y + dy + 4) % 4) * 4 + (x + dx + 4) % 4


def key_code(owner):
    _, y, x, core = place()
    dy, dx = (owner // 4 - y + 4) % 4, (owner % 4 - x + 4) % 4
    return jnp.where(core == 0, dx * 4 + dy, dy * 4 + dx)


def left_code(owner):
    here, _, _, core = place()
    offset = owner // 2 - here + 8
    return jnp.where(core == 0, offset, 16 - offset) % 8


def product(left, right):
    depth, width = right.shape[1:]
    l_re, l_im = left[0], left[1]
    both = jnp.concatenate([jnp.concatenate([l_re, -l_im], axis=1), jnp.concatenate([l_im, l_re], axis=1)], axis=0)
    value = jnp.dot(both, right.reshape(2 * depth, width), preferred_element_type=jnp.float32)
    return value.reshape(2, depth, width)


def pick_left(owner, lefts, keys, target, sem):
    depth = target.shape[-1]
    code = left_code(owner)
    start = pl.multiple_of((owner % 2) * depth, depth)
    for ref, key in zip(lefts, keys):
        @pl.when(code == key % 8)
        def _():
            pltpu.make_async_copy(ref.at[:, :, pl.ds(start, depth)], target, sem).start()


def early_kernel(*refs):
    refs = list(refs)
    lefts = [refs.pop(0) for _ in NEAR]
    rights = [refs.pop(0) for _ in EARLY]
    out, l_buf, r_buf, sems = refs
    owners = [owner_of(key) for key in EARLY]
    ready = [left_code(owner) != 4 for owner in owners]

    def start(k):
        @pl.when(ready[k])
        def _():
            pltpu.make_async_copy(rights[k], r_buf.at[k % 2], sems.at[k % 2, 0]).start()
        pick_left(owners[k], lefts, NEAR, l_buf.at[k % 2], sems.at[k % 2, 1])

    start(0)
    out[...] = jnp.zeros_like(out)
    for k in range(len(EARLY)):
        if k + 1 < len(EARLY):
            start(k + 1)

        @pl.when(ready[k])
        def _():
            pltpu.make_async_copy(rights[k], r_buf.at[k % 2], sems.at[k % 2, 0]).wait()
            pltpu.make_async_copy(lefts[0].at[:, :, pl.ds(0, l_buf.shape[-1])], l_buf.at[k % 2], sems.at[k % 2, 1]).wait()
            out[...] += product(l_buf[k % 2], r_buf[k % 2])


def late_kernel(scale, *refs):
    refs = list(refs)
    keys = NEAR + (4,)
    lefts = [refs.pop(0) for _ in keys]
    rights = [refs.pop(0) for _ in EARLY + LATE]
    total, out, l_buf, r_buf, sems = refs
    here = lax.axis_index("src")
    depth = l_buf.shape[-1]
    tasks = []
    for key in LATE:
        tasks.append((owner_of(key), None))
    for part in range(2):
        owner = 2 * ((here + 4) % 8) + part
        code = key_code(owner)
        tasks.append((owner, code))

    def is_early(code):
        hit = code == 0
        for a, b in EARLY[1:]:
            hit = jnp.logical_or(hit, code == (a % 4) * 4 + b % 4)
        return hit

    for k, (owner, code) in enumerate(tasks):
        if code is None:
            pltpu.make_async_copy(rights[len(EARLY) + k], r_buf.at[k], sems.at[k, 0]).start()
            pick_left(owner, lefts, keys, l_buf.at[k], sems.at[k, 1])
        else:
            for ref, (a, b) in zip(rights, EARLY):
                @pl.when(code == (a % 4) * 4 + b % 4)
                def _():
                    pltpu.make_async_copy(ref, r_buf.at[k], sems.at[k, 0]).start()
            start = pl.multiple_of((owner % 2) * depth, depth)
            pltpu.make_async_copy(lefts[-1].at[:, :, pl.ds(start, depth)], l_buf.at[k], sems.at[k, 1]).start()

    def finish(k, right=True):
        pltpu.make_async_copy(lefts[0].at[:, :, pl.ds(0, depth)], l_buf.at[k], sems.at[k, 1]).wait()

    out[...] = total[...]
    for k, (owner, code) in enumerate(tasks):
        pltpu.make_async_copy(lefts[0].at[:, :, pl.ds(0, depth)], l_buf.at[k], sems.at[k, 1]).wait()

        def work():
            pltpu.make_async_copy(rights[0], r_buf.at[k], sems.at[k, 0]).wait()
            out[...] += product(l_buf[k], r_buf[k])

        if code is None:
            work()
        else:
            pl.when(is_early(code))(work)
    out[...] *= scale


def call(kernel, operands, n_outside, slots, flops, depth, width, dtype):
    inside, outside = pl.BlockSpec(memory_space=pltpu.VMEM), pl.BlockSpec(memory_space=pl.ANY)
    return pl.pallas_call(
        kernel,
        out_shape=jax.ShapeDtypeStruct((2, depth, width), jnp.float32),
        in_specs=[outside] * n_outside + [inside] * (len(operands) - n_outside),
        out_specs=inside,
        scratch_shapes=[
            pltpu.VMEM((slots, 2, depth, depth), dtype),
            pltpu.VMEM((slots, 2, depth, width), dtype),
            pltpu.SemaphoreType.DMA((slots, 2)),
        ],
        compiler_params=pltpu.CompilerParams(vmem_limit_bytes=60 * 2**20),
        cost_estimate=pl.CostEstimate(flops=flops, bytes_accessed=n_outside * 2**20, transcendentals=0),
    )(*operands)


def per_device(slice_data):
    depth, width = slice_data.shape[1:]
    dtype = slice_data.dtype
    held = {(0, 0): slice_data, 0: slice_data}
    for i, (new, old, axis, hop) in enumerate(STEPS):
        value = held[old]
        if i >= WINDOW:
            past = STEPS[i - WINDOW][0]
            if past != old:
                value, held[past] = lax.optimization_barrier((value, held[past]))
        held[new] = move(value, axis, hop)

    unit = 8 * depth * depth * width
    early = [held[key] for key in list(NEAR) + EARLY]
    total = call(early_kernel, early, len(early), 2, unit * len(EARLY), depth, width, dtype)
    late = [held[key] for key in list(NEAR) + [4] + EARLY + LATE]
    kernel = functools.partial(late_kernel, 1.0 / float(NS) ** 0.5)
    return call(kernel, late + [total], len(late), len(LATE) + 2, unit * (len(LATE) + 2), depth, width, dtype)


def solution(mesh):
    in_specs = (P("freq", "rcv", "src"),)
    out_specs = P("freq", "rcv", "src")
    return jax.shard_map(
        per_device, mesh=mesh, in_specs=in_specs, out_specs=out_specs, check_vma=False
    )
```

```python
import functools

import jax
import jax.numpy as jnp
from jax import lax
from jax.experimental import pallas as pl
from jax.experimental.pallas import tpu as pltpu
from jax.sharding import PartitionSpec as P

NS = 6144
WINDOW = 5


def plane_pairs(first, hop):
    pairs = []
    for y in range(4):
        for x in range(4):
            for core in range(2):
                if (core == 0) == first:
                    target = y * 4 + (x + hop) % 4
                else:
                    target = ((y + hop) % 4) * 4 + x
                pairs.append(((y * 4 + x) * 2 + core, target * 2 + core))
    return pairs


def ring_pairs(hop):
    return [(z * 2 + core, (z + (hop if core == 0 else -hop)) % 8 * 2 + core) for z in range(8) for core in range(2)]


STEPS = (
    ((-1, 0), (0, 0), "a", 1),
    ((1, 0), (0, 0), "a", -1),
    (-1, 0, "z", 1),
    ((2, 0), (-1, 0), "a", 1),
    ((0, 1), (0, 0), "b", -1),
    (1, 0, "z", -1),
    ((0, -1), (0, 0), "b", 1),
    ((-1, 1), (-1, 0), "b", -1),
    (-2, -1, "z", 1),
    ((-1, -1), (-1, 0), "b", 1),
    ((1, 1), (1, 0), "b", -1),
    (2, 1, "z", -1),
    ((1, -1), (1, 0), "b", 1),
    ((0, 2), (0, 1), "b", -1),
    (-3, -2, "z", 1),
    ((2, -1), (2, 0), "b", 1),
    ((2, 1), (2, 0), "b", -1),
    (3, 2, "z", -1),
    ((-1, 2), (-1, -1), "b", 1),
    ((1, 2), (1, 1), "b", -1),
    (4, -3, "z", 1),
    ((2, 2), (2, -1), "b", 1),
)
EARLY = [(0, 0)] + [step[0] for step in STEPS[:18] if step[2] != "z"]
LATE = [step[0] for step in STEPS[18:] if step[2] != "z"]
NEAR = (0, 1, 2, 3, -3, -2, -1)


def move(value, axis, hop):
    if axis == "z":
        return lax.ppermute(value, ("src", "freq"), ring_pairs(hop))
    return lax.ppermute(value, ("rcv", "freq"), plane_pairs(axis == "a", hop))


def place():
    here, row, core = lax.axis_index("src"), lax.axis_index("rcv"), lax.axis_index("freq")
    return here, row // 4, row % 4, core


def owner_of(key):
    _, y, x, core = place()
    a, b = key
    dx, dy = jnp.where(core == 0, a, b), jnp.where(core == 0, b, a)
    return ((y + dy + 4) % 4) * 4 + (x + dx + 4) % 4


def key_code(owner):
    _, y, x, core = place()
    dy, dx = (owner // 4 - y + 4) % 4, (owner % 4 - x + 4) % 4
    return jnp.where(core == 0, dx * 4 + dy, dy * 4 + dx)


def left_code(owner):
    here, _, _, core = place()
    offset = owner // 2 - here + 8
    return jnp.where(core == 0, offset, 16 - offset) % 8


def product(left, right):
    depth, width = right.shape[1:]
    l_re, l_im = left[0], left[1]
    both = jnp.concatenate([jnp.concatenate([l_re, -l_im], axis=1), jnp.concatenate([l_im, l_re], axis=1)], axis=0)
    value = jnp.dot(both, right.reshape(2 * depth, width), preferred_element_type=jnp.float32)
    return value.reshape(2, depth, width)


def pick_left(owner, lefts, keys, target, sem):
    depth = target.shape[-1]
    code = left_code(owner)
    start = pl.multiple_of((owner % 2) * depth, depth)
    for ref, key in zip(lefts, keys):
        @pl.when(code == key % 8)
        def _():
            pltpu.make_async_copy(ref.at[:, :, pl.ds(start, depth)], target, sem).start()


def early_kernel(*refs):
    refs = list(refs)
    lefts = [refs.pop(0) for _ in NEAR]
    rights = [refs.pop(0) for _ in EARLY]
    out, l_buf, r_buf, sems, flags = refs
    owners = [owner_of(key) for key in EARLY]
    ready = [left_code(owner) != 4 for owner in owners]
    for k, hit in enumerate(ready):
        flags[k] = hit.astype(jnp.int32)

    def start(k):
        @pl.when(ready[k])
        def _():
            pltpu.make_async_copy(rights[k], r_buf.at[k % 2], sems.at[k % 2, 0]).start()
        pick_left(owners[k], lefts, NEAR, l_buf.at[k % 2], sems.at[k % 2, 1])

    start(0)
    out[...] = jnp.zeros_like(out)

    def step(k, carry):
        for j in range(1, len(EARLY)):
            @pl.when(k + 1 == j)
            def _():
                start(j)

        @pl.when(flags[k] == 1)
        def _():
            slot = lax.rem(k, 2)
            pltpu.make_async_copy(rights[0], r_buf.at[slot], sems.at[slot, 0]).wait()
            pltpu.make_async_copy(lefts[0].at[:, :, pl.ds(0, l_buf.shape[-1])], l_buf.at[slot], sems.at[slot, 1]).wait()
            out[...] += product(l_buf[slot], r_buf[slot])

        return carry

    lax.fori_loop(0, len(EARLY), step, 0)


def late_kernel(scale, *refs):
    refs = list(refs)
    keys = NEAR + (4,)
    lefts = [refs.pop(0) for _ in keys]
    rights = [refs.pop(0) for _ in EARLY + LATE]
    total, out, l_buf, r_buf, sems, flags = refs
    here = lax.axis_index("src")
    depth = l_buf.shape[-1]
    tasks = []
    for key in LATE:
        tasks.append((owner_of(key), None))
    for part in range(2):
        owner = 2 * ((here + 4) % 8) + part
        code = key_code(owner)
        tasks.append((owner, code))

    def is_early(code):
        hit = code == 0
        for a, b in EARLY[1:]:
            hit = jnp.logical_or(hit, code == (a % 4) * 4 + b % 4)
        return hit

    for k, (owner, code) in enumerate(tasks):
        if code is None:
            pltpu.make_async_copy(rights[len(EARLY) + k], r_buf.at[k], sems.at[k, 0]).start()
            pick_left(owner, lefts, keys, l_buf.at[k], sems.at[k, 1])
        else:
            for ref, (a, b) in zip(rights, EARLY):
                @pl.when(code == (a % 4) * 4 + b % 4)
                def _():
                    pltpu.make_async_copy(ref, r_buf.at[k], sems.at[k, 0]).start()
            start = pl.multiple_of((owner % 2) * depth, depth)
            pltpu.make_async_copy(lefts[-1].at[:, :, pl.ds(start, depth)], l_buf.at[k], sems.at[k, 1]).start()

    for k, (_, code) in enumerate(tasks):
        flags[k] = 1 if code is None else is_early(code).astype(jnp.int32)
    out[...] = total[...]

    def step(k, carry):
        pltpu.make_async_copy(lefts[0].at[:, :, pl.ds(0, depth)], l_buf.at[k], sems.at[k, 1]).wait()

        @pl.when(flags[k] == 1)
        def _():
            pltpu.make_async_copy(rights[0], r_buf.at[k], sems.at[k, 0]).wait()
            out[...] += product(l_buf[k], r_buf[k])

        return carry

    lax.fori_loop(0, len(tasks), step, 0)
    out[...] *= scale


def call(kernel, operands, n_outside, slots, flops, depth, width, dtype):
    inside, outside = pl.BlockSpec(memory_space=pltpu.VMEM), pl.BlockSpec(memory_space=pl.ANY)
    return pl.pallas_call(
        kernel,
        out_shape=jax.ShapeDtypeStruct((2, depth, width), jnp.float32),
        in_specs=[outside] * n_outside + [inside] * (len(operands) - n_outside),
        out_specs=inside,
        scratch_shapes=[
            pltpu.VMEM((slots, 2, depth, depth), dtype),
            pltpu.VMEM((slots, 2, depth, width), dtype),
            pltpu.SemaphoreType.DMA((slots, 2)),
            pltpu.SMEM((16,), jnp.int32),
        ],
        compiler_params=pltpu.CompilerParams(vmem_limit_bytes=60 * 2**20),
        cost_estimate=pl.CostEstimate(flops=flops, bytes_accessed=n_outside * 2**20, transcendentals=0),
    )(*operands)


def per_device(slice_data):
    depth, width = slice_data.shape[1:]
    dtype = slice_data.dtype
    held = {(0, 0): slice_data, 0: slice_data}
    for i, (new, old, axis, hop) in enumerate(STEPS):
        value = held[old]
        if i >= WINDOW:
            past = STEPS[i - WINDOW][0]
            if past != old:
                value, held[past] = lax.optimization_barrier((value, held[past]))
        held[new] = move(value, axis, hop)

    unit = 8 * depth * depth * width
    early = [held[key] for key in list(NEAR) + EARLY]
    total = call(early_kernel, early, len(early), 2, unit * len(EARLY), depth, width, dtype)
    late = [held[key] for key in list(NEAR) + [4] + EARLY + LATE]
    kernel = functools.partial(late_kernel, 1.0 / float(NS) ** 0.5)
    return call(kernel, late + [total], len(late), len(LATE) + 2, unit * (len(LATE) + 2), depth, width, dtype)


def solution(mesh):
    in_specs = (P("freq", "rcv", "src"),)
    out_specs = P("freq", "rcv", "src")
    return jax.shard_map(
        per_device, mesh=mesh, in_specs=in_specs, out_specs=out_specs, check_vma=False
    )
```

```python
import functools

import jax
import jax.numpy as jnp
from jax import lax
from jax.experimental import pallas as pl
from jax.experimental.pallas import tpu as pltpu
from jax.sharding import PartitionSpec as P

NS = 6144
WINDOW = 5
COLUMNS = 256


def plane_pairs(first, hop):
    pairs = []
    for y in range(4):
        for x in range(4):
            for core in range(2):
                if (core == 0) == first:
                    target = y * 4 + (x + hop) % 4
                else:
                    target = ((y + hop) % 4) * 4 + x
                pairs.append(((y * 4 + x) * 2 + core, target * 2 + core))
    return pairs


def ring_pairs(hop):
    return [(z * 2 + core, (z + (hop if core == 0 else -hop)) % 8 * 2 + core) for z in range(8) for core in range(2)]


STEPS = (
    ((-1, 0), (0, 0), "a", 1),
    ((1, 0), (0, 0), "a", -1),
    (-1, 0, "z", 1),
    ((2, 0), (-1, 0), "a", 1),
    ((0, 1), (0, 0), "b", -1),
    (1, 0, "z", -1),
    ((0, -1), (0, 0), "b", 1),
    ((-1, 1), (-1, 0), "b", -1),
    (-2, -1, "z", 1),
    ((-1, -1), (-1, 0), "b", 1),
    ((1, 1), (1, 0), "b", -1),
    (2, 1, "z", -1),
    ((1, -1), (1, 0), "b", 1),
    ((0, 2), (0, 1), "b", -1),
    (-3, -2, "z", 1),
    ((2, -1), (2, 0), "b", 1),
    ((2, 1), (2, 0), "b", -1),
    (3, 2, "z", -1),
    ((-1, 2), (-1, -1), "b", 1),
    ((1, 2), (1, 1), "b", -1),
    (4, -3, "z", 1),
    ((2, 2), (2, -1), "b", 1),
)
EARLY = [(0, 0)] + [step[0] for step in STEPS[:18] if step[2] != "z"]
LATE = [step[0] for step in STEPS[18:] if step[2] != "z"]
NEAR = (0, 1, 2, 3, -3, -2, -1)


def move(value, axis, hop):
    if axis == "z":
        return lax.ppermute(value, ("src", "freq"), ring_pairs(hop))
    return lax.ppermute(value, ("rcv", "freq"), plane_pairs(axis == "a", hop))


def place():
    here, row, core = lax.axis_index("src"), lax.axis_index("rcv"), lax.axis_index("freq")
    return here, row // 4, row % 4, core


def owner_of(key):
    _, y, x, core = place()
    a, b = key
    dx, dy = jnp.where(core == 0, a, b), jnp.where(core == 0, b, a)
    return ((y + dy + 4) % 4) * 4 + (x + dx + 4) % 4


def key_code(owner):
    _, y, x, core = place()
    dy, dx = (owner // 4 - y + 4) % 4, (owner % 4 - x + 4) % 4
    return jnp.where(core == 0, dx * 4 + dy, dy * 4 + dx)


def left_code(owner):
    here, _, _, core = place()
    offset = owner // 2 - here + 8
    return jnp.where(core == 0, offset, 16 - offset) % 8


def product(left, right):
    depth, width = right.shape[1:]
    l_re, l_im = left[0], left[1]
    both = jnp.concatenate([jnp.concatenate([l_re, -l_im], axis=1), jnp.concatenate([l_im, l_re], axis=1)], axis=0)
    value = jnp.dot(both, right.reshape(2 * depth, width), preferred_element_type=jnp.float32)
    return value.reshape(2, depth, width)


def pick_left(owner, lefts, keys, target, sem):
    depth = target.shape[-1]
    code = left_code(owner)
    start = pl.multiple_of((owner % 2) * depth, depth)
    for ref, key in zip(lefts, keys):
        @pl.when(code == key % 8)
        def _():
            pltpu.make_async_copy(ref.at[:, :, pl.ds(start, depth)], target, sem).start()


def early_kernel(*refs):
    refs = list(refs)
    lefts = [refs.pop(0) for _ in NEAR]
    rights = [refs.pop(0) for _ in EARLY]
    out, l_buf, r_buf, sems, flags = refs
    owners = [owner_of(key) for key in EARLY]
    ready = [left_code(owner) != 4 for owner in owners]
    for k, hit in enumerate(ready):
        flags[k] = hit.astype(jnp.int32)

    def start(k):
        @pl.when(ready[k])
        def _():
            pltpu.make_async_copy(rights[k], r_buf.at[k % 2], sems.at[k % 2, 0]).start()
        pick_left(owners[k], lefts, NEAR, l_buf.at[k % 2], sems.at[k % 2, 1])

    start(0)
    out[...] = jnp.zeros_like(out)

    def step(k, carry):
        for j in range(1, len(EARLY)):
            @pl.when(k + 1 == j)
            def _():
                start(j)

        @pl.when(flags[k] == 1)
        def _():
            slot = lax.rem(k, 2)
            pltpu.make_async_copy(rights[0], r_buf.at[slot], sems.at[slot, 0]).wait()
            pltpu.make_async_copy(lefts[0].at[:, :, pl.ds(0, l_buf.shape[-1])], l_buf.at[slot], sems.at[slot, 1]).wait()
            out[...] += product(l_buf[slot], r_buf[slot])

        return carry

    lax.fori_loop(0, len(EARLY), step, 0)


def late_kernel(scale, *refs):
    refs = list(refs)
    keys = NEAR + (4,)
    lefts = [refs.pop(0) for _ in keys]
    rights = [refs.pop(0) for _ in EARLY + LATE]
    total, out, l_buf, r_buf, sems, flags, acc = refs
    here = lax.axis_index("src")
    depth = l_buf.shape[-1]
    tasks = []
    for part in range(2):
        owner = 2 * ((here + 4) % 8) + part
        tasks.append((owner, key_code(owner)))
    for key in LATE:
        tasks.append((owner_of(key), None))

    def is_early(code):
        hit = code == 0
        for a, b in EARLY[1:]:
            hit = jnp.logical_or(hit, code == (a % 4) * 4 + b % 4)
        return hit

    for k, (owner, code) in enumerate(tasks):
        if code is None:
            pltpu.make_async_copy(rights[len(EARLY) + k - 2], r_buf.at[k], sems.at[k, 0]).start()
            pick_left(owner, lefts, keys, l_buf.at[k], sems.at[k, 1])
        else:
            for ref, (a, b) in zip(rights, EARLY):
                @pl.when(code == (a % 4) * 4 + b % 4)
                def _():
                    pltpu.make_async_copy(ref, r_buf.at[k], sems.at[k, 0]).start()
            start = pl.multiple_of((owner % 2) * depth, depth)
            pltpu.make_async_copy(lefts[-1].at[:, :, pl.ds(start, depth)], l_buf.at[k], sems.at[k, 1]).start()

    for k, (_, code) in enumerate(tasks):
        flags[k] = 1 if code is None else is_early(code).astype(jnp.int32)
    acc[...] = total[...]

    def step(k, carry):
        pltpu.make_async_copy(lefts[0].at[:, :, pl.ds(0, depth)], l_buf.at[k], sems.at[k, 1]).wait()

        @pl.when(flags[k] == 1)
        def _():
            pltpu.make_async_copy(rights[0], r_buf.at[k], sems.at[k, 0]).wait()
            acc[...] += product(l_buf[k], r_buf[k])

        return carry

    last = len(tasks) - 1
    lax.fori_loop(0, last, step, 0)
    pltpu.make_async_copy(lefts[0].at[:, :, pl.ds(0, depth)], l_buf.at[last], sems.at[last, 1]).wait()
    pltpu.make_async_copy(rights[0], r_buf.at[last], sems.at[last, 0]).wait()
    copies = []
    for k in range(3):
        tile = pl.ds(k * COLUMNS, COLUMNS)
        acc[:, :, tile] = (acc[:, :, tile] + product(l_buf[last], r_buf[last, :, :, tile])) * scale
        copies.append(pltpu.make_async_copy(acc.at[:, :, tile], out.at[:, :, tile], sems.at[k, 0]))
        copies[-1].start()
    for copy in copies:
        copy.wait()


def call(kernel, operands, n_outside, slots, flops, depth, width, dtype, extra=()):
    inside, outside = pl.BlockSpec(memory_space=pltpu.VMEM), pl.BlockSpec(memory_space=pl.ANY)
    return pl.pallas_call(
        kernel,
        out_shape=jax.ShapeDtypeStruct((2, depth, width), jnp.float32),
        in_specs=[outside] * n_outside + [inside] * (len(operands) - n_outside),
        out_specs=outside if extra else inside,
        scratch_shapes=[
            pltpu.VMEM((slots, 2, depth, depth), dtype),
            pltpu.VMEM((slots, 2, depth, width), dtype),
            pltpu.SemaphoreType.DMA((slots, 2)),
            pltpu.SMEM((16,), jnp.int32),
            *extra,
        ],
        compiler_params=pltpu.CompilerParams(vmem_limit_bytes=60 * 2**20),
        cost_estimate=pl.CostEstimate(flops=flops, bytes_accessed=n_outside * 2**20, transcendentals=0),
    )(*operands)


def per_device(slice_data):
    depth, width = slice_data.shape[1:]
    dtype = slice_data.dtype
    held = {(0, 0): slice_data, 0: slice_data}
    for i, (new, old, axis, hop) in enumerate(STEPS):
        value = held[old]
        if i >= WINDOW:
            past = STEPS[i - WINDOW][0]
            if past != old:
                value, held[past] = lax.optimization_barrier((value, held[past]))
        held[new] = move(value, axis, hop)

    unit = 8 * depth * depth * width
    early = [held[key] for key in list(NEAR) + EARLY]
    total = call(early_kernel, early, len(early), 2, unit * len(EARLY), depth, width, dtype)
    late = [held[key] for key in list(NEAR) + [4] + EARLY + LATE]
    kernel = functools.partial(late_kernel, 1.0 / float(NS) ** 0.5)
    return call(kernel, late + [total], len(late), len(LATE) + 2, unit * (len(LATE) + 2), depth, width, dtype, [pltpu.VMEM((2, depth, width), jnp.float32)])


def solution(mesh):
    in_specs = (P("freq", "rcv", "src"),)
    out_specs = P("freq", "rcv", "src")
    return jax.shard_map(
        per_device, mesh=mesh, in_specs=in_specs, out_specs=out_specs, check_vma=False
    )
```
